32 devices in a mesh: fsdp: 4 (over y, x), ctx: 8 (over z, core).
Axes of the slice: x: 2, y: 2, z: 4, core: 2. Of those that a mesh axis runs over, the one named last changes fastest.
Arguments:
- block_input: bfloat16 [8, 2048, 960], P('fsdp', 'ctx'), may hold values from -6 to 6
- query_weight: bfloat16 [960, 960], P('fsdp'), may hold values from -0.1875 to 0.1875
- key_matrix: bfloat16 [960, 320], P('fsdp'), may hold values from -0.1875 to 0.1875
- value_matrix: bfloat16 [960, 320], P('fsdp'), may hold values from -0.1875 to 0.1875
- out_weight: bfloat16 [960, 960], P('fsdp'), may hold values from -1.5 to 1.5
- gate_weight: bfloat16 [960, 2560], P('fsdp'), may hold values from -0.1875 to 0.1875
- up_weight: bfloat16 [960, 2560], P('fsdp'), may hold values from -0.1875 to 0.1875
- down_weight: bfloat16 [2560, 960], P('fsdp'), may hold values from -0.125 to 0.125
- attention_gain: bfloat16 [960], P('fsdp'), may hold values from 0.5 to 1.5
- feedforward_gain: bfloat16 [960], P('fsdp'), may hold values from 0.5 to 1.5
- cotangent: bfloat16 [8, 2048, 960], P('fsdp', 'ctx'), may hold values from -6 to 6
Outputs:
- block_output: bfloat16 [8, 2048, 960], P('fsdp', 'ctx')
- input_grad: bfloat16 [8, 2048, 960], P('fsdp', 'ctx')
- query_grad: float32 [960, 960], P('fsdp')
- key_grad: float32 [960, 320], P('fsdp')
- value_grad: float32 [960, 320], P('fsdp')
- out_grad: float32 [960, 960], P('fsdp')
- gate_grad: float32 [960, 2560], P('fsdp')
- up_grad: float32 [960, 2560], P('fsdp')
- down_grad: float32 [2560, 960], P('fsdp')
- attention_gain_grad: float32 [960], P('fsdp')
- feedforward_gain_grad: float32 [960], P('fsdp')
The draws below stay inside these ranges and needn't reach their ends.
All inputs are finite; a program needn't handle non-finite values.
Results may differ from the reference program's by a relative error of at most 0.024.
Values may be sent and summed in bfloat16 or wider, within the bound.
No kernel may reach another device: no remote copies, remote signals or barrier semaphores. Data moves between devices by JAX's collectives and lax.ppermute only.
A program may use at most 192 MiB of HBM per device.

```python
import math
import jax
import jax.numpy as jnp
from jax import lax

MODEL_DIM = 960
QUERY_HEAD_COUNT = 15
KEY_HEAD_COUNT = 5
HEAD_DIM = 64
FF = 2560
SEQS = 8
LEN = 2048


def level_of(own_key, shape, split, low, top_value):
    def one(dim, blocks):
        heights = jax.random.uniform(jax.random.fold_in(jax.random.fold_in(own_key, 6), dim), (blocks,), jnp.float32, low / len(split), top_value / len(split))
        return jnp.repeat(jnp.exp(heights), shape[dim] // blocks).reshape((-1,) + (1,) * (len(shape) - dim - 1))

    level = one(*split[0])
    for cut in split[1:]:
        level = level * one(*cut)
    return level


def centred(stream_key, dims, width, most, split=(), kind=jnp.bfloat16):
    array = jax.random.normal(stream_key, dims, jnp.float32) * width
    if len(split) > 0:
        array = level_of(stream_key, dims, split, -0.22, 0.18) * array
    return jnp.clip(array, min=-most, max=most).astype(kind)


def setup_inputs(seed: int = 0) -> dict:
    key_of = jax.random.split(jax.random.key(seed), 12)
    block_input = centred(key_of[0], (SEQS, LEN, MODEL_DIM), 1.0, 6.0, ((0, 4), (1, 8)))
    query_weight = centred(key_of[1], (MODEL_DIM, QUERY_HEAD_COUNT * HEAD_DIM), MODEL_DIM ** -0.5, 0.1875, ((0, 4),))
    key_matrix = centred(key_of[2], (MODEL_DIM, KEY_HEAD_COUNT * HEAD_DIM), MODEL_DIM ** -0.5, 0.1875, ((0, 4),))
    value_matrix = centred(key_of[3], (MODEL_DIM, KEY_HEAD_COUNT * HEAD_DIM), MODEL_DIM ** -0.5, 0.1875, ((0, 4),))
    out_weight = centred(key_of[4], (QUERY_HEAD_COUNT * HEAD_DIM, MODEL_DIM), (max(QUERY_HEAD_COUNT * HEAD_DIM // 64, 1)) ** -0.5, 1.5, ((0, 4),))
    gate_weight = centred(key_of[5], (MODEL_DIM, FF), MODEL_DIM ** -0.5, 0.1875, ((0, 4),))
    up_weight = centred(key_of[6], (MODEL_DIM, FF), MODEL_DIM ** -0.5, 0.1875, ((0, 4),))
    down_weight = centred(key_of[7], (FF, MODEL_DIM), FF ** -0.5, 0.125, ((0, 4),))
    attention_gain = jnp.clip(1.0 + 0.1 * jax.random.normal(key_of[8], (MODEL_DIM,), jnp.float32), 0.5, 1.5).astype(jnp.bfloat16)
    feedforward_gain = jnp.clip(1.0 + 0.1 * jax.random.normal(key_of[9], (MODEL_DIM,), jnp.float32), 0.5, 1.5).astype(jnp.bfloat16)
    cotangent = centred(key_of[10], (SEQS, LEN, MODEL_DIM), 1.0, 6.0, ((0, 4), (1, 8)))
    return {"block_input": block_input, "query_weight": query_weight, "key_matrix": key_matrix, "value_matrix": value_matrix, "out_weight": out_weight, "gate_weight": gate_weight, "up_weight": up_weight, "down_weight": down_weight, "attention_gain": attention_gain, "feedforward_gain": feedforward_gain, "cotangent": cotangent}


@jax.custom_vjp
def lower_dtype(v):
    return lax.optimization_barrier(v.astype(jnp.bfloat16)).astype(jnp.float32)

@jax.custom_vjp
def lower_dtype_return(v):
    return v

def low_keep(v):
    return (lower_dtype(v), None)

def low_pass(kept, grad):
    return (grad,)

def back_keep(v):
    return (v, None)

def back_low(kept, grad):
    return (lower_dtype(grad),)
lower_dtype.defvjp(low_keep, low_pass)
lower_dtype_return.defvjp(back_keep, back_low)
eps_norm = 1e-05
rope_base = 100000.0
masked_score = -1e+30
highest_precision = lax.Precision.HIGHEST

def rope_tables(positions, head_width):
    steps_half = jnp.arange(head_width // 2, dtype=jnp.float32)
    frequencies = rope_base ** (-2.0 * steps_half / head_width)
    angles = positions.astype(jnp.float32)[:, None] * frequencies[None, :]
    angles = jnp.concatenate([angles, angles], axis=-1)
    return (jnp.cos(angles), jnp.sin(angles))

def turn_half(field):
    middle_index = field.shape[-1] // 2
    return jnp.concatenate([-field[..., middle_index:], field[..., :middle_index]], axis=-1)

def apply_rotation(field, cosine_table, sine_table):
    return field * cosine_table + turn_half(field) * sine_table

def apply_norm(field, scale_gain):
    inverse = lax.rsqrt(lax.optimization_barrier(jnp.mean(field * field, axis=-1, keepdims=True)) + eps_norm)
    return field * inverse * scale_gain

def attend_block(first_row, query_head_rows, key_head_rows, value_head_rows):
    sequence_length = key_head_rows.shape[0]
    block_rows = math.gcd(sequence_length, 512)
    query_rows = lax.dynamic_slice_in_dim(query_head_rows, first_row, block_rows, 0)
    scores = lower_dtype_return(jnp.einsum('qhd,khd->hqk', query_rows, key_head_rows, precision=highest_precision) * 0.125)
    row_pos = first_row + jnp.arange(block_rows, dtype=jnp.int32)
    col_pos = jnp.arange(sequence_length, dtype=jnp.int32)
    allowed = col_pos[None, :] <= row_pos[:, None]
    scores = jnp.where(allowed[None], scores, masked_score)
    weights = lower_dtype(jax.nn.softmax(scores, axis=-1))
    return jnp.einsum('hqk,khd->qhd', weights, value_head_rows, precision=highest_precision)

def forward(block_input, query_weight, key_matrix, value_matrix, out_weight, gate_weight, up_weight, down_weight, attention_gain, feedforward_gain):
    sequence_length = block_input.shape[0]
    cosine_table, sine_table = rope_tables(jnp.arange(sequence_length, dtype=jnp.int32), HEAD_DIM)
    first_normed = lower_dtype(apply_norm(block_input, attention_gain))
    query_lin = lower_dtype_return(jnp.dot(first_normed, query_weight, precision=highest_precision)).reshape(sequence_length, QUERY_HEAD_COUNT, HEAD_DIM)
    key_linear = lower_dtype_return(jnp.dot(first_normed, key_matrix, precision=highest_precision)).reshape(sequence_length, KEY_HEAD_COUNT, HEAD_DIM)
    value_head_rows = lower_dtype(lower_dtype_return(jnp.dot(first_normed, value_matrix, precision=highest_precision))).reshape(sequence_length, KEY_HEAD_COUNT, HEAD_DIM)
    query_head_rows = lower_dtype(apply_rotation(query_lin, cosine_table[:, None, :], sine_table[:, None, :]))
    key_head_rows = lower_dtype(apply_rotation(key_linear, cosine_table[:, None, :], sine_table[:, None, :]))
    key_head_rows = jnp.repeat(key_head_rows, QUERY_HEAD_COUNT // KEY_HEAD_COUNT, axis=1)
    value_head_rows = jnp.repeat(value_head_rows, QUERY_HEAD_COUNT // KEY_HEAD_COUNT, axis=1)
    block_rows = math.gcd(sequence_length, 512)
    first_rows = jnp.arange(sequence_length // block_rows, dtype=jnp.int32) * block_rows
    checked = jax.checkpoint(attend_block)

    def one_block(first_row):
        return checked(first_row, query_head_rows, key_head_rows, value_head_rows)
    attended = lax.map(one_block, first_rows).reshape(sequence_length, QUERY_HEAD_COUNT * HEAD_DIM)
    attended = lower_dtype(lower_dtype_return(attended))
    middle = block_input + lower_dtype_return(jnp.dot(attended, out_weight, precision=highest_precision))
    normed_two = lower_dtype(apply_norm(middle, feedforward_gain))
    gate_lin = lower_dtype_return(jnp.dot(normed_two, gate_weight, precision=highest_precision))
    up_lin = lower_dtype_return(jnp.dot(normed_two, up_weight, precision=highest_precision))
    hidden = lower_dtype(jax.nn.silu(gate_lin) * up_lin)
    return middle + lower_dtype_return(jnp.dot(hidden, down_weight, precision=highest_precision))

def reference(block_input, query_weight, key_matrix, value_matrix, out_weight, gate_weight, up_weight, down_weight, attention_gain, feedforward_gain, cotangent):
    params = tuple((item.astype(jnp.float32) for item in (query_weight, key_matrix, value_matrix, out_weight, gate_weight, up_weight, down_weight, attention_gain, feedforward_gain)))

    def one_sequence(carry, item):
        seq_input, seq_cotangent = item
        result, pull = jax.vjp(forward, seq_input.astype(jnp.float32), *params)
        grads = pull(seq_cotangent.astype(jnp.float32))
        carry = tuple((left + right for left, right in zip(carry, grads[1:])))
        return (carry, (result.astype(jnp.bfloat16), grads[0].astype(jnp.bfloat16)))
    initial = tuple((jnp.zeros(item.shape, jnp.float32) for item in params))
    totals, (outputs, input_grads) = lax.scan(one_sequence, initial, (block_input, cotangent))
    return (outputs, input_grads, totals[0], totals[1], totals[2], totals[3], totals[4], totals[5], totals[6], totals[7], totals[8])
```

```python
import functools

import jax
import jax.numpy as jnp
from jax import lax
from jax.experimental import pallas as pl
from jax.experimental.pallas import tpu as pltpu
from jax.sharding import PartitionSpec as P

QUERY_HEAD_COUNT = 15
KEY_HEAD_COUNT = 5
HEAD_DIM = 64
GROUP = QUERY_HEAD_COUNT // KEY_HEAD_COUNT

eps_norm = 1e-05
rope_base = 100000.0
masked_score = -1e30

f32 = jnp.float32
bf16 = jnp.bfloat16
AXES = ("fsdp", "ctx")
VMEM_BYTES = 48 * 1024 * 1024

NN = ((1,), (0,))
NT = ((1,), (1,))
TN = ((0,), (0,))


def dot(a, b, dims=NN):
    return lax.dot_general(a, b, (dims, ((), ())), preferred_element_type=f32)


def call(kernel, outs, args, flops, scratch=(), smem=0, hbm=(), outs_hbm=(), trans=0):
    specs = []
    for k in range(len(args)):
        if k < smem:
            specs.append(pl.BlockSpec(memory_space=pltpu.SMEM))
        elif k in hbm:
            specs.append(pl.BlockSpec(memory_space=pl.ANY))
        else:
            specs.append(pl.BlockSpec(memory_space=pltpu.VMEM))
    shapes = [jax.ShapeDtypeStruct(s, d) for s, d in outs]
    moved = sum(a.size * a.dtype.itemsize for a in args) + sum(
        s.size * s.dtype.itemsize for s in shapes
    )
    return pl.pallas_call(
        kernel,
        out_shape=shapes,
        in_specs=specs,
        out_specs=[
            pl.BlockSpec(memory_space=pl.ANY if k in outs_hbm else pltpu.VMEM)
            for k in range(len(shapes))
        ],
        scratch_shapes=list(scratch),
        compiler_params=pltpu.CompilerParams(vmem_limit_bytes=VMEM_BYTES),
        cost_estimate=pl.CostEstimate(
            flops=int(flops), bytes_accessed=int(moved), transcendentals=int(trans)
        ),
    )(*args)


def rotate_rows(part, cos, sin):
    half = HEAD_DIM // 2
    a, b = part[:half], part[half:]
    return jnp.concatenate([a * cos - b * sin, b * cos + a * sin], axis=0)


def unrotate_rows(part, cos, sin):
    half = HEAD_DIM // 2
    a, b = part[:half], part[half:]
    return jnp.concatenate([a * cos + b * sin, b * cos - a * sin], axis=0)


def run_copies(pairs, sems):
    copies = [pltpu.make_async_copy(a, b, sems.at[k]) for k, (a, b) in enumerate(pairs)]
    for copy in copies:
        copy.start()
    return copies


def placed(pieces, dst, order_ref, base, rows):
    pairs = []
    for s, piece in enumerate(pieces):
        if len(pieces) == 1:
            pairs.append((piece, dst))
        else:
            at = pl.multiple_of(order_ref[base + s] * rows, 16)
            pairs.append((piece.at[pl.ds(0, rows)], dst.at[pl.ds(at, rows)]))
    return pairs


def key_kernel(parts, slots, order_ref, x_ref, cos_ref, sin_ref, *refs):
    mine, theirs = refs[:parts], refs[parts : 2 * parts]
    refs = refs[2 * parts :]
    if parts == 1:
        gain_in, refs = refs[0], refs[1:]
    n1_ref, kv_ref, w_ref, gain_ref, gain_scr, sems = refs
    core = order_ref[0]
    width = x_ref.shape[1]
    rows = width // parts
    pairs = placed(mine, w_ref.at[core], order_ref, 1 + core * slots, rows)
    pairs += placed(theirs, w_ref.at[1 - core], order_ref, 1 + (1 - core) * slots, rows)
    if parts > 1:
        for s, piece in enumerate(mine):
            pairs.append((piece.at[pl.ds(rows, 16)], gain_scr.at[order_ref[1 + core * slots + s]]))
    copies = run_copies(pairs, sems)
    x = x_ref[...].astype(f32)
    inv = lax.rsqrt(jnp.mean(x * x, axis=-1, keepdims=True) + eps_norm)
    cos, sin = cos_ref[...], sin_ref[...]
    for copy in copies:
        copy.wait()
    if parts > 1:
        both = jnp.concatenate(
            [gain_scr[j].astype(f32)[:8, :rows] for j in range(parts)], axis=1
        )
    else:
        both = gain_in[...]
    gain_ref[...] = both
    n1_ref[...] = (x * inv * both[0:1, :]).astype(bf16)
    n1 = n1_ref[...]
    lin_t = dot(n1, w_ref[0]).T
    turned = [
        rotate_rows(lin_t[HEAD_DIM * h : HEAD_DIM * (h + 1)], cos, sin)
        for h in range(KEY_HEAD_COUNT)
    ]
    keys = jnp.concatenate(turned, axis=0).T.astype(bf16)
    values = dot(n1, w_ref[1]).astype(bf16)
    kv_ref[...] = jnp.concatenate([keys, values], axis=1)


def query_kernel(parts, slots, order_ref, n1_ref, cos_ref, sin_ref, *refs):
    mine, theirs = refs[:parts], refs[parts : 2 * parts]
    qt_ref, q_ref, wq_ref, wo_ref, sems = refs[2 * parts :]
    core = order_ref[0]
    rows = n1_ref.shape[1] // parts

    for c in range(2):

        @pl.when(core == c)
        def _():
            mine_to, theirs_to = (wq_ref, wo_ref) if c == 0 else (wo_ref, wq_ref)
            pairs = placed(mine, mine_to, order_ref, 1 + c * slots, rows)
            pairs += placed(theirs, theirs_to, order_ref, 1 + (1 - c) * slots, rows)
            for copy in run_copies(pairs, sems):
                copy.wait()

    cos, sin = cos_ref[...], sin_ref[...]
    lin_t = dot(n1_ref[...], wq_ref[...]).T
    for h in range(QUERY_HEAD_COUNT):
        turned = rotate_rows(lin_t[HEAD_DIM * h : HEAD_DIM * (h + 1)], cos, sin) * 0.125
        qt_ref[h] = turned.astype(bf16)
        q_ref[h] = turned.T.astype(bf16)


def halves_kernel(slots, order_ref, gate_ref, up_ref, down_ref, gu_ref, d_ref):
    ff = gate_ref.shape[1]
    step = ff // slots
    half = step // 2
    for c in range(2):

        @pl.when(order_ref[0] == c)
        def _():
            for j in range(slots):
                src = slice(step * j + half * c, step * j + half * (c + 1))
                gu_ref[:, half * j : half * (j + 1)] = gate_ref[:, src]
                gu_ref[:, ff // 2 + half * j : ff // 2 + half * (j + 1)] = up_ref[:, src]
            d_ref[...] = down_ref[half * c : half * (c + 1), :]


def forward_diagonal(qt_ref, kv_ref, m_ref, l_ref, acc_ref, k_scr, vt_scr):
    keys = kv_ref.shape[0]
    for g in range(KEY_HEAD_COUNT):
        k_scr[g] = kv_ref[:, HEAD_DIM * g : HEAD_DIM * (g + 1)]
        start = HEAD_DIM * (KEY_HEAD_COUNT + g)
        vt_scr[g] = kv_ref[:, start : start + HEAD_DIM].astype(f32).T.astype(bf16)
    m_ref[...] = jnp.zeros_like(m_ref)
    l_ref[...] = jnp.ones_like(l_ref)
    half = keys // 2

    @pl.loop(0, KEY_HEAD_COUNT)
    def _(g):
        for i in range(GROUP):
            h = g * GROUP + i
            for part in range(2):
                cols = slice(part * half, (part + 1) * half)
                used = (part + 1) * half
                st = dot(k_scr[g, :used, :], qt_ref[h, :, cols])
                key_at = lax.broadcasted_iota(jnp.int32, st.shape, 0)
                row_at = lax.broadcasted_iota(jnp.int32, st.shape, 1) + part * half
                st = jnp.where(key_at <= row_at, st, masked_score)
                top = jnp.max(st, axis=0, keepdims=True)
                p = jnp.exp(st - top)
                m_ref[g, i : i + 1, cols] = top
                l_ref[g, i : i + 1, cols] = jnp.sum(p, axis=0, keepdims=True)
                acc_ref[h, :, cols] = dot(vt_scr[g, :, :used], p.astype(bf16))


def forward_full(
    ok_ref, qt_ref, kv_ref, m_in, l_in, acc_in, m_ref, l_ref, acc_ref, k_scr, vt_scr
):
    m_ref[...] = m_in[...]
    l_ref[...] = l_in[...]

    @pl.when(ok_ref[0] == 0)
    def _():
        acc_ref[...] = acc_in[...]

    @pl.when(ok_ref[0] != 0)
    def _():
        for g in range(KEY_HEAD_COUNT):
            k_scr[g] = kv_ref[:, HEAD_DIM * g : HEAD_DIM * (g + 1)]
            start = HEAD_DIM * (KEY_HEAD_COUNT + g)
            vt_scr[g] = kv_ref[:, start : start + HEAD_DIM].astype(f32).T.astype(bf16)

        @pl.loop(0, KEY_HEAD_COUNT)
        def _(g):
            for i in range(GROUP):
                h = g * GROUP + i
                st = dot(k_scr[g], qt_ref[h])
                old = m_in[g, i : i + 1, :]
                top = jnp.maximum(old, jnp.max(st, axis=0, keepdims=True))
                factor = jnp.exp(old - top)
                p = jnp.exp(st - top)
                m_ref[g, i : i + 1, :] = top
                l_ref[g, i : i + 1, :] = l_in[g, i : i + 1, :] * factor + jnp.sum(
                    p, axis=0, keepdims=True
                )
                acc_ref[h] = acc_in[h] * factor + dot(vt_scr[g], p.astype(bf16))


def middle_kernel(x_ref, acc_ref, l_ref, wo_ref, gain_ref, att_ref, mid_ref, n2_ref):
    for h in range(QUERY_HEAD_COUNT):
        g, i = divmod(h, GROUP)
        att_ref[HEAD_DIM * h : HEAD_DIM * (h + 1), :] = (
            acc_ref[h] / l_ref[g, i : i + 1, :]
        ).astype(bf16)
    middle = x_ref[...].astype(f32) + dot(att_ref[...], wo_ref[...], TN)
    mid_ref[...] = middle
    inv = lax.rsqrt(jnp.mean(middle * middle, axis=-1, keepdims=True) + eps_norm)
    n2_ref[...] = (middle * inv * gain_ref[1:2, :]).astype(bf16)


def ff_kernel(parts, slots, groups, tile, order_ref, *refs):
    gu_pieces, d_pieces = refs[:parts], refs[parts : 2 * parts]
    n2m_ref, n2t_ref, cot_ref = refs[2 * parts : 2 * parts + 3]
    refs = refs[2 * parts + 3 :]
    out_ref, gn_ref, send_ref = refs[:3]
    gu_outs, d_outs = refs[3 : 3 + groups], refs[3 + groups : 3 + 2 * groups]
    wgu, wd, n2, turned, out, gn, ggu, gd, sems, out_sems = refs[3 + 2 * groups :]
    core = order_ref[0]
    width, ff2 = wgu.shape
    ff = ff2 // 2
    rows = n2m_ref.shape[0]
    base = 1 + core * slots
    copies = run_copies(
        placed(gu_pieces, wgu, order_ref, base, width // parts)
        + placed(d_pieces, wd, order_ref, base, ff // parts),
        sems,
    )
    n2[:rows, :] = n2m_ref[...]
    n2[rows:, :] = n2t_ref[...]
    turned[:, :rows] = n2m_ref[...].astype(f32).T.astype(bf16)
    turned[:, rows:] = n2t_ref[...].astype(f32).T.astype(bf16)
    out[...] = jnp.zeros_like(out)
    gn[...] = jnp.zeros_like(gn)
    for copy in copies:
        copy.wait()
    shard = width // slots

    @pl.loop(0, ff // tile)
    def _(step):
        at = pl.multiple_of(step * tile, tile)
        up_at = pl.multiple_of(ff + step * tile, 128)
        wg = wgu[:, pl.ds(at, tile)]
        wu = wgu[:, pl.ds(up_at, tile)]
        w_down = wd[pl.ds(at, tile), :]
        cot = cot_ref[...]
        gate = dot(n2[...], wg)
        up = dot(n2[...], wu)
        s = jax.nn.sigmoid(gate)
        swish = gate * s
        hidden = (swish * up).astype(bf16)
        grad_hidden = dot(cot, w_down, NT)
        grad_gate = (grad_hidden * up * s * (1.0 + gate * (1.0 - s))).astype(bf16)
        grad_up = (grad_hidden * swish).astype(bf16)
        out[...] += dot(hidden, w_down)
        gn[...] += dot(grad_gate, wg, NT) + dot(grad_up, wu, NT)
        gd[pl.ds(at, tile), :] = dot(hidden, cot, TN).astype(bf16)
        g_gate = dot(turned[...], grad_gate).astype(bf16)
        g_up = dot(turned[...], grad_up).astype(bf16)
        for j in range(slots):
            slot = order_ref[1 + (2 + core) * slots + j]
            ggu[slot, :, pl.ds(at, tile)] = g_gate[shard * j : shard * (j + 1)]
            ggu[slot, :, pl.ds(up_at, tile)] = g_up[shard * j : shard * (j + 1)]

    per = slots // groups
    down_rows = ff // slots
    pairs = [(ggu.at[pl.ds(per * k, per)], gu_outs[k]) for k in range(groups)]
    for s in range(slots):
        at = pl.multiple_of(order_ref[base + s] * down_rows, 16)
        pairs.append((gd.at[pl.ds(at, down_rows)], d_outs[s // per].at[s % per]))
    copies = run_copies(pairs, out_sems)
    out_ref[...] = out[:rows, :]
    gn_ref[...] = gn[:rows, :]
    send_ref[:, :width] = out[rows:, :].astype(bf16)
    send_ref[:, width:] = gn[rows:, :].astype(bf16)
    for copy in copies:
        copy.wait()


def turn_kernel(
    slots, order_ref, mid_ref, sum_ref, gn_ref, got_ref, gain_ref, cot_ref, wo_ref, att_ref,
    acc_ref, m_ref, l_ref,
    fin_ref, gm_ref, og_ref, og_send_ref, do_ref, dot_ref, del_ref, lse_ref, gg_ref,
):
    core = order_ref[0]
    middle = mid_ref[...]
    width = middle.shape[1]
    fin_ref[...] = (middle + sum_ref[...] + got_ref[:, :width].astype(f32)).astype(bf16)
    inv = lax.rsqrt(jnp.mean(middle * middle, axis=-1, keepdims=True) + eps_norm)
    gn = gn_ref[...] + got_ref[:, width:].astype(f32)
    gg_ref[...] = jnp.sum(gn * middle * inv, axis=0, keepdims=True)
    u = gn * gain_ref[1:2, :]
    gm = cot_ref[...].astype(f32) + inv * u - middle * (inv * inv * inv) * jnp.mean(
        u * middle, axis=-1, keepdims=True
    )
    gm_ref[...] = gm
    low = gm.astype(bf16)
    shard = width // slots
    split = og_ref.shape[2]
    og = dot(att_ref[...], low)
    for part in range(2):
        piece = og[:, :split] if part == 0 else og[:, split:]
        wide = piece.shape[1]
        for keep in range(2):
            ref = og_ref if keep else og_send_ref

            @pl.when((core == part) == (keep == 1))
            def _():
                if wide < split:
                    ref[:, :, wide:] = jnp.zeros((slots, shard, split - wide), bf16)
                for j in range(slots):
                    slot = order_ref[1 + (2 + part) * slots + j]
                    ref[slot, :, :wide] = piece[shard * j : shard * (j + 1)].astype(bf16)

    ga_t = dot(wo_ref[...], low, NT)
    del_ref[...] = jnp.zeros_like(del_ref)
    lse_ref[...] = m_ref[...] + jnp.log(l_ref[...])
    for h in range(QUERY_HEAD_COUNT):
        g, i = divmod(h, GROUP)
        part = ga_t[HEAD_DIM * h : HEAD_DIM * (h + 1)].astype(bf16)
        dot_ref[h] = part
        wide = part.astype(f32)
        do_ref[h] = wide.T.astype(bf16)
        del_ref[g, i : i + 1, :] = jnp.sum(
            wide * (acc_ref[h] / l_ref[g, i : i + 1, :]), axis=0, keepdims=True
        )


def backward_kernel(diagonal, first, *refs):
    if first:
        ok_ref, qt_ref, q_ref, dot_ref, do_ref, lse_ref, del_ref, kv_ref, dq_ref, dkv_ref, *scr = refs
        dq_in = None
    else:
        (
            ok_ref, qt_ref, q_ref, dot_ref, do_ref, lse_ref, del_ref, kv_ref, dq_in, dq_ref, dkv_ref, *scr,
        ) = refs
    k_scr, v_scr, kt_scr, dk_scr, dv_scr = scr
    keys = kv_ref.shape[0]

    @pl.when(ok_ref[0] == 0)
    def _():
        dq_ref[...] = jnp.zeros_like(dq_ref) if first else dq_in[...]
        dkv_ref[...] = jnp.zeros_like(dkv_ref)

    @pl.when(ok_ref[0] != 0)
    def _():
        for g in range(KEY_HEAD_COUNT):
            k = kv_ref[:, HEAD_DIM * g : HEAD_DIM * (g + 1)]
            k_scr[g] = k
            kt_scr[g] = k.astype(f32).T.astype(bf16)
            start = HEAD_DIM * (KEY_HEAD_COUNT + g)
            v_scr[g] = kv_ref[:, start : start + HEAD_DIM]

        parts = 2 if diagonal else 1
        rows = q_ref.shape[1]

        @pl.loop(0, KEY_HEAD_COUNT)
        def _(g):
            for part in range(parts):
                cols = slice(part * rows // parts, (part + 1) * rows // parts)
                used = (part + 1) * rows // parts if diagonal else keys
                dk = dv = None
                for i in range(GROUP):
                    h = g * GROUP + i
                    st = dot(k_scr[g, :used, :], qt_ref[h, :, cols])
                    p = jnp.exp(st - lse_ref[g, i : i + 1, cols])
                    if diagonal:
                        key_at = lax.broadcasted_iota(jnp.int32, st.shape, 0)
                        row_at = lax.broadcasted_iota(jnp.int32, st.shape, 1) + cols.start
                        p = jnp.where(key_at <= row_at, p, 0.0)
                    dpt = dot(v_scr[g, :used, :], dot_ref[h, :, cols])
                    ds = (p * (dpt - del_ref[g, i : i + 1, cols])).astype(bf16)
                    more_v = dot(p.astype(bf16), do_ref[h, cols, :])
                    more_k = dot(ds, q_ref[h, cols, :])
                    dv = more_v if dv is None else dv + more_v
                    dk = more_k if dk is None else dk + more_k
                    more_q = dot(kt_scr[g, :, :used], ds)
                    if first:
                        dq_ref[h, :, cols] = more_q
                    else:
                        dq_ref[h, :, cols] = dq_in[h, :, cols] + more_q
                if part == 0:
                    dk_scr[g, :used, :] = dk
                    dv_scr[g, :used, :] = dv
                else:
                    before = part * rows // parts
                    dk_scr[g, :before, :] += dk[:before]
                    dv_scr[g, :before, :] += dv[:before]
                    dk_scr[g, before:used, :] = dk[before:]
                    dv_scr[g, before:used, :] = dv[before:]

        dkv_ref[...] = jnp.concatenate(
            [dk_scr[g].astype(bf16) for g in range(KEY_HEAD_COUNT)]
            + [dv_scr[g].astype(bf16) for g in range(KEY_HEAD_COUNT)],
            axis=1,
        )


def last_kernel(
    slots, order_ref, dq_ref, dkv_ref, got_ref, n1_ref, wq_ref, w_ref, cos_ref, sin_ref, x_ref,
    gain_ref, gm_ref, gg_two_ref,
    ig_ref, keep_ref, send_ref, dqt_scr, n1t_scr, rhs_scr, gg_scr,
):
    core = order_ref[0]
    cos, sin = cos_ref[...], sin_ref[...]
    for h in range(QUERY_HEAD_COUNT):
        dqt_scr[HEAD_DIM * h : HEAD_DIM * (h + 1), :] = unrotate_rows(
            dq_ref[h] * 0.125, cos, sin
        ).astype(bf16)
    n1t_scr[...] = n1_ref[...].astype(f32).T.astype(bf16)
    n1t = n1t_scr[...]
    dqt = dqt_scr[...]
    width = dqt.shape[0]
    kv_width = KEY_HEAD_COUNT * HEAD_DIM
    cut = 2 * kv_width + width
    cut = keep_ref.shape[2]
    first = width - (cut - 2 * kv_width)
    dkv = dkv_ref[...].astype(f32) + got_ref[...].astype(f32)
    dk_t = dkv[:, :kv_width].T
    turned = [
        unrotate_rows(dk_t[HEAD_DIM * h : HEAD_DIM * (h + 1)], cos, sin)
        for h in range(KEY_HEAD_COUNT)
    ]
    dk = jnp.concatenate(turned, axis=0).T.astype(bf16)
    dv = dkv[:, kv_width:].astype(bf16)
    dq = dqt.astype(f32).T.astype(bf16)
    rhs_scr[:, : 2 * kv_width] = jnp.concatenate([dk, dv], axis=1)
    rhs_scr[:, 2 * kv_width :] = dq[:, first:]
    gn = dot(dq, wq_ref[...], NT) + dot(dk, w_ref[0], NT) + dot(dv, w_ref[1], NT)
    x = x_ref[...].astype(f32)
    inv = lax.rsqrt(jnp.mean(x * x, axis=-1, keepdims=True) + eps_norm)
    gg_one = jnp.sum(gn * x * inv, axis=0, keepdims=True)
    w = gn * gain_ref[0:1, :]
    ig_ref[...] = (
        gm_ref[...]
        + inv * w
        - x * (inv * inv * inv) * jnp.mean(w * x, axis=-1, keepdims=True)
    ).astype(bf16)
    shard = width // slots
    extra = keep_ref.shape[1] - shard
    row_at = lax.broadcasted_iota(jnp.int32, (extra, shard), 0)
    for j in range(slots):
        cols = slice(shard * j, shard * (j + 1))
        gg_scr[j, :, :] = jnp.zeros(gg_scr.shape[1:], f32)
        gg_scr[j, :, :shard] = jnp.where(
            row_at == 0, gg_one[:, cols], jnp.where(row_at == 1, gg_two_ref[:, cols], 0.0)
        )
    for part in range(2):
        if part == 0:
            piece = dot(n1t, dqt[:first], NT)
        else:
            piece = dot(n1t, rhs_scr[...])
        wide = piece.shape[1]
        for keep in range(2):
            ref = keep_ref if keep else send_ref

            @pl.when((core == part) == (keep == 1))
            def _():
                if wide < cut:
                    ref[:, :, wide:] = jnp.zeros((slots, shard + extra, cut - wide), bf16)
                for j in range(slots):
                    slot = order_ref[1 + (2 + part) * slots + j]
                    block = piece[shard * j : shard * (j + 1)]
                    tail = gg_scr[j] if part == 0 else jnp.zeros(gg_scr.shape[1:], f32)
                    ref[slot, :, :wide] = jnp.concatenate(
                        [block, tail[:, :wide]], axis=0
                    ).astype(bf16)


def finish_ff_kernel(
    slots, order_ref, gum_ref, gut_ref, dm_ref, dt_ref, om_ref, ot_ref,
    gate_ref, up_ref, down_ref, o_ref,
):
    ff = gate_ref.shape[1]
    step = ff // slots
    half = step // 2
    split = om_ref.shape[1]
    for core in range(2):

        @pl.when(order_ref[0] == core)
        def _():
            for c in range(2):
                gu, d, o = (gum_ref, dm_ref, om_ref) if c == core else (gut_ref, dt_ref, ot_ref)
                for j in range(slots):
                    dst = slice(step * j + half * c, step * j + half * (c + 1))
                    src = slice(half * j, half * (j + 1))
                    gate_ref[:, dst] = gu[:, src].astype(f32)
                    src = slice(ff // 2 + half * j, ff // 2 + half * (j + 1))
                    up_ref[:, dst] = gu[:, src].astype(f32)
                down_ref[half * c : half * (c + 1), :] = d[...].astype(f32)
                if c == 0:
                    o_ref[:, :split] = o[...].astype(f32)
                else:
                    o_ref[:, split:] = o[:, : o_ref.shape[1] - split].astype(f32)


def finish_kernel(chips, order_ref, *refs):
    mine, theirs = refs[:chips], refs[chips : 2 * chips]
    qg_ref, kg_ref, vg_ref, gg_ref, parts_scr = refs[2 * chips :]
    core = order_ref[0]
    place = order_ref[1]
    step = mine[0].shape[0]
    for k in range(chips):
        at = pl.multiple_of(lax.rem(place + chips - k, chips) * step, 16)
        parts_scr[core, pl.ds(at, step), :] = mine[k][...]
        parts_scr[1 - core, pl.ds(at, step), :] = theirs[k][...]
    shard, width = qg_ref.shape
    kv_width = kg_ref.shape[1]
    cut = parts_scr.shape[2]
    first = width - (cut - 2 * kv_width)
    qg_ref[:, :first] = parts_scr[0, :shard, :first].astype(f32)
    qg_ref[:, first:] = parts_scr[1, :shard, 2 * kv_width :].astype(f32)
    kg_ref[...] = parts_scr[1, :shard, :kv_width].astype(f32)
    vg_ref[...] = parts_scr[1, :shard, kv_width : 2 * kv_width].astype(f32)
    gg_ref[...] = parts_scr[0].astype(f32)[shard : shard + 8, :shard]


def moves(fsdp, ctx, target):
    pairs = []
    for f in range(fsdp):
        for c in range(ctx):
            to_f, to_c = target(f, c)
            if 0 <= to_c < ctx:
                pairs.append((f * ctx + c, to_f * ctx + to_c))
    return pairs


def plus(a, b):
    return (a.astype(f32) + b.astype(f32)).astype(bf16)


def program(
    fsdp, ctx,
    block_input, query_weight, key_matrix, value_matrix, out_weight, gate_weight, up_weight,
    down_weight, attention_gain, feedforward_gain, cotangent,
):
    chips = ctx // 2
    paired = fsdp == 4
    sibling = moves(fsdp, ctx, lambda f, c: (f, c ^ 1))
    up_z = moves(fsdp, ctx, lambda f, c: (f, c + 2))
    down_z = moves(fsdp, ctx, lambda f, c: (f, c - 2))
    near = moves(fsdp, ctx, lambda f, c: (f ^ (1 + c % 2), c))
    far = moves(fsdp, ctx, lambda f, c: (f ^ (2 - c % 2), c))
    rotations = [
        moves(fsdp, ctx, lambda f, c, k=k: (f, (c + 2 * k) % ctx)) for k in range(chips)
    ]
    columns = [[c + 2 * z for z in range(chips)] for c in range(2)]
    rank = lax.axis_index("ctx")
    core, place = rank % 2, rank // 2
    spot = lax.axis_index("fsdp")
    _, half, width = block_input.shape
    rows = 2 * half
    kv_width = KEY_HEAD_COUNT * HEAD_DIM
    shard = width // fsdp
    ff = gate_weight.shape[1]
    parts = fsdp if paired else 1

    def send(value, pairs):
        return lax.ppermute(value, AXES, pairs)

    ids = jnp.arange(fsdp, dtype=jnp.int32)
    if paired:
        first_order = jnp.bitwise_xor(spot, ids)
        swapped = jnp.array([0, 2, 1, 3], jnp.int32)
        second_order = jnp.bitwise_xor(spot, swapped)
        flip = jnp.bitwise_xor(spot, ids)
        second_slot = jnp.where(flip == 1, 2, jnp.where(flip == 2, 1, flip))
        order = [core[None], first_order, second_order, first_order, second_slot]
    else:
        order = [core[None], ids, ids, ids, ids]
    order = jnp.concatenate([o.astype(jnp.int32) for o in order])

    def gather(item):
        if not paired:
            return [lax.all_gather(item, "fsdp", axis=0, tiled=True)]
        a = send(item, near)
        b = send(item, far)
        return [item, a, b, send(a, far)]

    def swap_pieces(pieces, own):
        if not paired:
            return [send(pieces[0], sibling)]
        return [own] + [send(piece, sibling) for piece in pieces[1:]]

    def gather_pair(one, two):
        mine = gather(jnp.where(core == 0, one, two))
        return mine, swap_pieces(mine, jnp.where(core == 0, two, one))

    x_keep = lax.dynamic_index_in_dim(block_input, core, 0, keepdims=False)
    x_send = lax.dynamic_index_in_dim(block_input, 1 - core, 0, keepdims=False)
    x_got = send(x_send, sibling)
    x = jnp.concatenate(
        [jnp.where(core == 0, x_keep, x_got), jnp.where(core == 0, x_got, x_keep)], axis=0
    )

    def scatter_sequence(block):
        keep = lax.dynamic_slice_in_dim(block, core * half, half, 0)
        got = send(lax.dynamic_slice_in_dim(block, (1 - core) * half, half, 0), sibling)
        return jnp.stack([jnp.where(core == 0, keep, got), jnp.where(core == 0, got, keep)])

    positions = (place * rows + jnp.arange(rows, dtype=jnp.int32)).astype(f32)
    steps = jnp.arange(HEAD_DIM // 2, dtype=f32)
    angles = (rope_base ** (-2.0 * steps / HEAD_DIM))[:, None] * positions[None, :]
    cos, sin = jnp.cos(angles), jnp.sin(angles)

    if paired:
        gains = jnp.pad(
            jnp.stack([attention_gain, feedforward_gain]), ((0, 14), (0, kv_width - shard))
        )
        mine, theirs = gather_pair(
            jnp.concatenate([key_matrix, gains], axis=0),
            jnp.concatenate([value_matrix, gains], axis=0),
        )
        gain_args = ()
    else:
        mine, theirs = gather_pair(key_matrix, value_matrix)
        gains = jnp.stack([attention_gain, feedforward_gain])
        gains = lax.all_gather(gains.astype(f32), "fsdp", axis=1, tiled=True)
        gain_args = (jnp.pad(gains, ((0, 6), (0, 0))),)
    n1, kv, w_kv, gain = call(
        functools.partial(key_kernel, parts, fsdp),
        [
            ((rows, width), bf16),
            ((rows, 2 * kv_width), bf16),
            ((2, width, kv_width), bf16),
            ((8, width), f32),
        ],
        (order, x, cos, sin, *mine, *theirs, *gain_args),
        2 * rows * width * 2 * kv_width,
        scratch=[pltpu.VMEM((parts, 16, kv_width), bf16), pltpu.SemaphoreType.DMA((3 * parts,))],
        smem=1,
        hbm=range(4, 4 + 2 * parts),
    )

    blocks = [kv]
    for _ in range(1, chips):
        blocks.append(send(blocks[-1], up_z))

    mine, theirs = gather_pair(query_weight, out_weight)
    qt, q, wq, wo = call(
        functools.partial(query_kernel, parts, fsdp),
        [
            ((QUERY_HEAD_COUNT, HEAD_DIM, rows), bf16),
            ((QUERY_HEAD_COUNT, rows, HEAD_DIM), bf16),
            ((width, width), bf16),
            ((width, width), bf16),
        ],
        (order, n1, cos, sin, *mine, *theirs),
        2 * rows * width * width,
        scratch=[pltpu.SemaphoreType.DMA((2 * parts,))],
        smem=1,
        hbm=range(4, 4 + 2 * parts),
    )

    gate_up, down_half = call(
        functools.partial(halves_kernel, fsdp),
        [((shard, ff), bf16), ((down_weight.shape[0] // 2, width), bf16)],
        (order, gate_weight, up_weight, down_weight),
        0,
        smem=1,
    )
    gate_up = gather(gate_up)
    down_half = gather(down_half)

    stat = ((KEY_HEAD_COUNT, 8, rows), f32)
    acc_shape = ((QUERY_HEAD_COUNT, HEAD_DIM, rows), f32)
    key_scratch = pltpu.VMEM((KEY_HEAD_COUNT, rows, HEAD_DIM), bf16)
    turned_scratch = pltpu.VMEM((KEY_HEAD_COUNT, HEAD_DIM, rows), bf16)
    wide_scratch = pltpu.VMEM((KEY_HEAD_COUNT, rows, HEAD_DIM), f32)
    score_flops = 2 * rows * rows * width
    exps = rows * rows * QUERY_HEAD_COUNT

    def ok(distance):
        return (place >= distance).astype(jnp.int32)[None]

    m, l, acc = call(
        forward_diagonal,
        [stat, stat, acc_shape],
        (qt, kv),
        1.5 * score_flops,
        scratch=[key_scratch, turned_scratch],
        trans=exps,
    )
    for distance in range(1, chips):
        m, l, acc = call(
            forward_full,
            [stat, stat, acc_shape],
            (ok(distance), qt, blocks[distance], m, l, acc),
            2 * score_flops,
            scratch=[key_scratch, turned_scratch],
            smem=1,
            trans=exps,
        )

    att, middle, n2 = call(
        middle_kernel,
        [((width, rows), bf16), ((rows, width), f32), ((rows, width), bf16)],
        (x, acc, l, wo, gain),
        2 * rows * width * width,
    )

    n2_got = send(n2, sibling)
    cot_got = send(cotangent, sibling)
    cot_first = jnp.where(core == 0, cotangent, cot_got)
    cot_second = jnp.where(core == 0, cot_got, cotangent)
    cot_first = jnp.where(core == 0, cot_first, cot_first[::-1])
    cot_second = jnp.where(core == 0, cot_second, cot_second[::-1])
    cot = jnp.concatenate([cot_first, cot_second], axis=1).reshape(2 * rows, width)
    groups = 2 if paired else 1
    per = fsdp // groups
    half_ff = ff // 2
    down_rows = half_ff // fsdp
    tile = 256
    ff_out = call(
        functools.partial(ff_kernel, parts, fsdp, groups, tile),
        [((rows, width), f32), ((rows, width), f32), ((rows, 2 * width), bf16)]
        + [((per, shard, ff), bf16)] * groups
        + [((per, down_rows, width), bf16)] * groups,
        (order, *gate_up, *down_half, n2, n2_got, cot),
        18 * rows * width * ff,
        scratch=[
            pltpu.VMEM((width, ff), bf16),
            pltpu.VMEM((half_ff, width), bf16),
            pltpu.VMEM((2 * rows, width), bf16),
            pltpu.VMEM((width, 2 * rows), bf16),
            pltpu.VMEM((2 * rows, width), f32),
            pltpu.VMEM((2 * rows, width), f32),
            pltpu.VMEM((fsdp, shard, ff), bf16),
            pltpu.VMEM((half_ff, width), bf16),
            pltpu.SemaphoreType.DMA((2 * parts,)),
            pltpu.SemaphoreType.DMA((groups + fsdp,)),
        ],
        smem=1,
        hbm=range(1, 1 + 2 * parts),
        outs_hbm=range(3, 3 + 2 * groups),
        trans=2 * rows * half_ff,
    )
    ff_sum, gn, ff_send = ff_out[:3]
    gu_terms, down_terms = ff_out[3 : 3 + groups], ff_out[3 + groups :]
    ff_got = send(ff_send, sibling)

    split = 512
    final, grad_middle, o_keep, o_send, do, dot_t, delta, lse, gain_two_term = call(
        functools.partial(turn_kernel, fsdp),
        [
            ((rows, width), bf16),
            ((rows, width), f32),
            ((fsdp, shard, split), bf16),
            ((fsdp, shard, split), bf16),
            ((QUERY_HEAD_COUNT, rows, HEAD_DIM), bf16),
            ((QUERY_HEAD_COUNT, HEAD_DIM, rows), bf16),
            stat,
            stat,
            ((1, width), f32),
        ],
        (order, middle, ff_sum, gn, ff_got, gain, cot[:rows], wo, att, acc, m, l),
        4 * rows * width * width,
        smem=1,
    )

    def reduce_rows(terms):
        if not paired:
            return lax.psum_scatter(terms[0], "fsdp", scatter_dimension=0, tiled=False)
        total = plus(terms[0], send(terms[1], far))
        return plus(total[0], send(total[1], near))

    def grouped(term):
        return [term[per * k : per * (k + 1)] for k in range(groups)]

    gu_part = reduce_rows(gu_terms)
    down_part = reduce_rows(down_terms)
    o_part = reduce_rows(grouped(plus(o_keep, send(o_send, sibling))))
    gu_part, down_part, o_part = lax.psum(
        (gu_part, down_part, o_part), "ctx", axis_index_groups=columns
    )

    dq = None
    coming = None
    for distance in reversed(range(chips)):
        first = dq is None
        args = (ok(distance), qt, q, dot_t, do, lse, delta, blocks[distance])
        dq, dkv = call(
            functools.partial(backward_kernel, distance == 0, first),
            [acc_shape, ((rows, 2 * kv_width), bf16)],
            args if first else args + (dq,),
            5 * score_flops,
            scratch=[key_scratch, key_scratch, turned_scratch, wide_scratch, wide_scratch],
            smem=1,
            trans=exps,
        )
        if distance > 0:
            coming = send(dkv if coming is None else plus(dkv, coming), down_z)

    step = 16 * chips
    tail_rows = -(-(shard + 8) // step) * step
    cut = 832
    input_grad, keep, other = call(
        functools.partial(last_kernel, fsdp),
        [
            ((rows, width), bf16),
            ((fsdp, tail_rows, cut), bf16),
            ((fsdp, tail_rows, cut), bf16),
        ],
        (order, dq, dkv, coming, n1, wq, w_kv, cos, sin, x, gain, grad_middle, gain_two_term),
        4 * rows * width * (width + 2 * kv_width),
        scratch=[
            pltpu.VMEM((width, rows), bf16),
            pltpu.VMEM((width, rows), bf16),
            pltpu.VMEM((rows, cut), bf16),
            pltpu.VMEM((fsdp, tail_rows - shard, cut), f32),
        ],
        smem=1,
    )
    part = reduce_rows(grouped(plus(keep, send(other, sibling))))

    block = tail_rows // chips
    total = lax.dynamic_slice_in_dim(part, place * block, block, 0).astype(f32)
    for k in range(1, chips):
        to = (place + k) % chips
        piece = lax.dynamic_slice_in_dim(part, to * block, block, 0)
        total = total + send(piece, rotations[k]).astype(f32)
    total = total.astype(bf16)
    pieces = [total] + [send(total, rotations[k]) for k in range(1, chips)]
    other_pieces = [send(piece, sibling) for piece in pieces]
    query_grad, key_grad, value_grad, gain_grads = call(
        functools.partial(finish_kernel, chips),
        [
            ((shard, width), f32),
            ((shard, kv_width), f32),
            ((shard, kv_width), f32),
            ((8, shard), f32),
        ],
        (jnp.stack([core, place]).astype(jnp.int32), *pieces, *other_pieces),
        0,
        scratch=[pltpu.VMEM((2, tail_rows, cut), bf16)],
        smem=1,
    )
    gate_grad, up_grad, down_grad, out_grad = call(
        functools.partial(finish_ff_kernel, fsdp),
        [
            ((shard, ff), f32),
            ((shard, ff), f32),
            ((ff // fsdp, width), f32),
            ((shard, width), f32),
        ],
        (
            order, gu_part, send(gu_part, sibling), down_part, send(down_part, sibling),
            o_part, send(o_part, sibling),
        ),
        0,
        smem=1,
    )

    return (
        scatter_sequence(final),
        scatter_sequence(input_grad),
        query_grad,
        key_grad,
        value_grad,
        out_grad,
        gate_grad,
        up_grad,
        down_grad,
        gain_grads[0],
        gain_grads[1],
    )


def solution(mesh):
    in_specs = (
        P("fsdp", "ctx", None),
        P("fsdp", None),
        P("fsdp", None),
        P("fsdp", None),
        P("fsdp", None),
        P("fsdp", None),
        P("fsdp", None),
        P("fsdp", None),
        P("fsdp"),
        P("fsdp"),
        P("fsdp", "ctx", None),
    )
    out_specs = (
        P("fsdp", "ctx", None),
        P("fsdp", "ctx", None),
        P("fsdp", None),
        P("fsdp", None),
        P("fsdp", None),
        P("fsdp", None),
        P("fsdp", None),
        P("fsdp", None),
        P("fsdp", None),
        P("fsdp"),
        P("fsdp"),
    )
    body = functools.partial(program, mesh.shape["fsdp"], mesh.shape["ctx"])
    return jax.shard_map(body, mesh=mesh, in_specs=in_specs, out_specs=out_specs, check_vma=False)
```

```python
import functools

import jax
import jax.numpy as jnp
from jax import lax
from jax.experimental import pallas as pl
from jax.experimental.pallas import tpu as pltpu
from jax.sharding import PartitionSpec as P

QUERY_HEAD_COUNT = 15
KEY_HEAD_COUNT = 5
HEAD_DIM = 64
GROUP = QUERY_HEAD_COUNT // KEY_HEAD_COUNT

eps_norm = 1e-05
rope_base = 100000.0
masked_score = -1e30

f32 = jnp.float32
bf16 = jnp.bfloat16
AXES = ("fsdp", "ctx")
SMALL = 32 * 1024 * 1024
LARGE = 60 * 1024 * 1024

NN = ((1,), (0,))
NT = ((1,), (1,))
TN = ((0,), (0,))


def dot(a, b, dims=NN):
    return lax.dot_general(a, b, (dims, ((), ())), preferred_element_type=f32)


def call(kernel, outs, args, micros, scratch=(), smem=0, hbm=(), outs_hbm=(), after=(), vmem=SMALL):
    count = len(args)
    specs = []
    for k in range(count):
        if k < smem:
            specs.append(pl.BlockSpec(memory_space=pltpu.SMEM))
        elif k in hbm:
            specs.append(pl.BlockSpec(memory_space=pl.ANY))
        else:
            specs.append(pl.BlockSpec(memory_space=pltpu.VMEM))
    specs += [pl.BlockSpec(memory_space=pl.ANY)] * len(after)
    shapes = [jax.ShapeDtypeStruct(s, d) for s, d in outs]

    def body(*refs):
        kernel(*refs[:count], *refs[count + len(after) :])

    return pl.pallas_call(
        body,
        out_shape=shapes,
        in_specs=specs,
        out_specs=[
            pl.BlockSpec(memory_space=pl.ANY if k in outs_hbm else pltpu.VMEM)
            for k in range(len(shapes))
        ],
        scratch_shapes=list(scratch),
        compiler_params=pltpu.CompilerParams(vmem_limit_bytes=vmem),
        cost_estimate=pl.CostEstimate(
            flops=int(micros * 1.15e9), bytes_accessed=0, transcendentals=0
        ),
    )(*args, *after)


def call_grid(kernel, steps, outs, args, micros, scratch=(), after=(), vmem=SMALL):
    scalars, args = args[0], args[1:]
    count = len(args)

    def body(*refs):
        kernel(*refs[: count + 1], *refs[count + 1 + len(after) :])

    return pl.pallas_call(
        body,
        out_shape=[jax.ShapeDtypeStruct(shape, kind) for (shape, kind), _, _ in outs],
        grid_spec=pltpu.PrefetchScalarGridSpec(
            num_scalar_prefetch=1,
            grid=(steps,),
            in_specs=[pl.BlockSpec(block, index) for _, block, index in args]
            + [pl.BlockSpec(memory_space=pl.ANY)] * len(after),
            out_specs=[pl.BlockSpec(block, index) for _, block, index in outs],
            scratch_shapes=list(scratch),
        ),
        compiler_params=pltpu.CompilerParams(
            dimension_semantics=("arbitrary",), vmem_limit_bytes=vmem
        ),
        cost_estimate=pl.CostEstimate(
            flops=int(micros * 1.15e9), bytes_accessed=0, transcendentals=0
        ),
    )(scalars, *[a for a, _, _ in args], *after)


def whole(array):
    rank = len(array.shape)
    return (array, array.shape, lambda i, s: (0,) * rank)


def leading(array, size):
    rank = len(array.shape)
    return (array, (size, *array.shape[1:]), lambda i, s: (i,) + (0,) * (rank - 1))


def trailing(array, size):
    rank = len(array.shape)
    return (array, (*array.shape[:-1], size), lambda i, s: (0,) * (rank - 1) + (i,))


class Out:
    def __init__(self, shape, kind):
        self.shape, self.kind = shape, kind

    def __iter__(self):
        return iter((self.shape, self.kind))


def rotate_rows(part, cos, sin):
    half = HEAD_DIM // 2
    a, b = part[:half], part[half:]
    return jnp.concatenate([a * cos - b * sin, b * cos + a * sin], axis=0)


def unrotate_rows(part, cos, sin):
    half = HEAD_DIM // 2
    a, b = part[:half], part[half:]
    return jnp.concatenate([a * cos + b * sin, b * cos - a * sin], axis=0)


def run_copies(pairs, sems):
    copies = [pltpu.make_async_copy(a, b, sems.at[k]) for k, (a, b) in enumerate(pairs)]
    for copy in copies:
        copy.start()
    return copies


def placed(pieces, dst, order_ref, base, rows):
    pairs = []
    for s, piece in enumerate(pieces):
        if len(pieces) == 1:
            pairs.append((piece, dst))
        else:
            at = pl.multiple_of(order_ref[base + s] * rows, 16)
            pairs.append((piece.at[pl.ds(0, rows)], dst.at[pl.ds(at, rows)]))
    return pairs


def inverse_norm(field):
    return lax.rsqrt(jnp.mean(field * field, axis=0, keepdims=True) + eps_norm)


def norm_back(grad_normed, field, inverse, scale_gain):
    scaled = grad_normed * scale_gain
    gain_term = jnp.sum(grad_normed * field * inverse, axis=1, keepdims=True)
    grad_field = inverse * scaled - field * (inverse * inverse * inverse) * jnp.mean(
        scaled * field, axis=0, keepdims=True
    )
    return grad_field, gain_term


def first_kernel(order_ref, x_ref, k_ref, v_ref, gain_ref, item_ref, send_ref, sem):
    core = order_ref[0]
    copy = pltpu.make_async_copy(x_ref.at[1 - core], send_ref, sem)
    copy.start()
    wide = k_ref.shape[0]

    @pl.when(core == 0)
    def _():
        item_ref[:wide, :] = k_ref[...]

    @pl.when(core == 1)
    def _():
        item_ref[:wide, :] = v_ref[...]

    item_ref[wide:, :] = gain_ref[...]
    copy.wait()


def key_kernel(parts, slots, order_ref, x_ref, got_ref, cos_ref, sin_ref, *refs):
    mine, theirs = refs[:parts], refs[parts : 2 * parts]
    xt_ref, n1t_ref, kv_ref, w_ref, gain_ref, sems = refs[2 * parts :]
    core = order_ref[0]
    width, tokens = xt_ref.shape
    rows = width // parts
    half = tokens // 2
    pairs = [
        (x_ref.at[core], xt_ref.at[:, pl.ds(pl.multiple_of(core * half, 128), half)]),
        (got_ref, xt_ref.at[:, pl.ds(pl.multiple_of((1 - core) * half, 128), half)]),
    ]
    for s in range(parts):
        j = order_ref[1 + core * slots + s] if parts > 1 else 0
        pairs.append((mine[s], w_ref.at[core, j]))
    for s in range(parts):
        j = order_ref[1 + (1 - core) * slots + s] if parts > 1 else 0
        pairs.append((theirs[s], w_ref.at[1 - core, j]))
    copies = run_copies(pairs, sems)
    for copy in copies:
        copy.wait()
    x = xt_ref[...].astype(f32)
    inv = inverse_norm(x)
    kv_width = KEY_HEAD_COUNT * HEAD_DIM
    for j in range(parts):
        gain_ref[rows * j : rows * (j + 1), :] = w_ref[0, j, kv_width:, :].astype(f32).T[:, :8]
    n1t_ref[...] = (x * inv * gain_ref[:, 0:1]).astype(bf16)
    cos, sin = cos_ref[...], sin_ref[...]
    lin = []
    for c in range(2):
        total = None
        for j in range(parts):
            more = dot(w_ref[c, j, :kv_width, :], n1t_ref[rows * j : rows * (j + 1), :])
            total = more if total is None else total + more
        lin.append(total)
    turned = [
        rotate_rows(lin[0][HEAD_DIM * h : HEAD_DIM * (h + 1)], cos, sin)
        for h in range(KEY_HEAD_COUNT)
    ]
    kv_ref[...] = jnp.concatenate(turned + [lin[1]], axis=0).T.astype(bf16)


def query_kernel(parts, slots, order_ref, n1t_ref, cos_ref, sin_ref, *refs):
    mine, theirs = refs[:parts], refs[parts : 2 * parts]
    qt_ref, q_ref, wq_ref, wo_ref, sems = refs[2 * parts :]
    core = order_ref[0]
    rows = n1t_ref.shape[0] // parts

    for c in range(2):

        @pl.when(core == c)
        def _():
            mine_to, theirs_to = (wq_ref, wo_ref) if c == 0 else (wo_ref, wq_ref)
            pairs = placed(mine, mine_to, order_ref, 1 + c * slots, rows)
            pairs += placed(theirs, theirs_to, order_ref, 1 + (1 - c) * slots, rows)
            for copy in run_copies(pairs, sems):
                copy.wait()

    cos, sin = cos_ref[...], sin_ref[...]
    lin_t = dot(wq_ref[...], n1t_ref[...], TN)
    for h in range(QUERY_HEAD_COUNT):
        turned = rotate_rows(lin_t[HEAD_DIM * h : HEAD_DIM * (h + 1)], cos, sin) * 0.125
        qt_ref[h] = turned.astype(bf16)
        q_ref[h] = turned.T.astype(bf16)


def pack_down(block, rows):
    rest = block.shape[0] - rows
    count = rows // rest
    cols = block.shape[1] // count
    extra = [block[rows:, cols * k : cols * (k + 1)] for k in range(count)]
    return jnp.concatenate([block[:rows], jnp.concatenate(extra, axis=0)], axis=1)


def unpack_down(packed, width):
    rows = packed.shape[0]
    cols = packed.shape[1] - width
    count = width // cols
    rest = rows // count
    extra = [packed[rest * k : rest * (k + 1), width:] for k in range(count)]
    return jnp.concatenate([packed[:, :width], jnp.concatenate(extra, axis=1)], axis=0)


def halves_kernel(slots, order_ref, q_ref, o_ref, gate_ref, up_ref, down_ref, qo_ref, gu_ref, d_ref):
    ff = gate_ref.shape[1]
    step = ff // slots
    half = step // 2
    for c in range(2):

        @pl.when(order_ref[0] == c)
        def _():
            qo_ref[...] = q_ref[...] if c == 0 else o_ref[...]
            for j in range(slots):
                src = slice(step * j + half * c, step * j + half * (c + 1))
                gu_ref[:, half * j : half * (j + 1)] = gate_ref[:, src]
                gu_ref[:, ff // 2 + half * j : ff // 2 + half * (j + 1)] = up_ref[:, src]
            d_ref[...] = down_ref[:, half * c : half * (c + 1)].astype(f32).T.astype(bf16)


def split_values(kv_ref, k_scr, vt_scr):
    for g in range(KEY_HEAD_COUNT):
        k_scr[g] = kv_ref[:, HEAD_DIM * g : HEAD_DIM * (g + 1)]
        start = HEAD_DIM * (KEY_HEAD_COUNT + g)
        vt_scr[g] = kv_ref[:, start : start + HEAD_DIM].astype(f32).T.astype(bf16)


def forward_diagonal(ok_ref, qt_ref, kv_ref, m_ref, l_ref, acc_ref, k_scr, vt_scr):
    g = pl.program_id(0)

    @pl.when(g == 0)
    def _():
        split_values(kv_ref, k_scr, vt_scr)

    half = kv_ref.shape[0] // 2
    m_ref[...] = jnp.zeros_like(m_ref)
    l_ref[...] = jnp.ones_like(l_ref)
    for i in range(GROUP):
        for part in range(2):
            cols = slice(part * half, (part + 1) * half)
            used = (part + 1) * half
            st = dot(k_scr[g, :used, :], qt_ref[i, :, cols])
            key_at = lax.broadcasted_iota(jnp.int32, st.shape, 0)
            row_at = lax.broadcasted_iota(jnp.int32, st.shape, 1) + part * half
            st = jnp.where(key_at <= row_at, st, masked_score)
            top = jnp.max(st, axis=0, keepdims=True)
            p = jnp.exp(st - top)
            m_ref[0, i : i + 1, cols] = top
            l_ref[0, i : i + 1, cols] = jnp.sum(p, axis=0, keepdims=True)
            acc_ref[i, :, cols] = dot(vt_scr[g, :, :used], p.astype(bf16))


def forward_full(
    ok_ref, qt_ref, kv_ref, m_in, l_in, acc_in, m_ref, l_ref, acc_ref, k_scr, vt_scr
):
    g = pl.program_id(0)
    m_ref[...] = m_in[...]
    l_ref[...] = l_in[...]

    @pl.when(ok_ref[0] == 0)
    def _():
        acc_ref[...] = acc_in[...]

    @pl.when(ok_ref[0] != 0)
    def _():
        @pl.when(g == 0)
        def _():
            split_values(kv_ref, k_scr, vt_scr)

        for i in range(GROUP):
            st = dot(k_scr[g], qt_ref[i])
            old = m_in[0, i : i + 1, :]
            top = jnp.maximum(old, jnp.max(st, axis=0, keepdims=True))
            factor = jnp.exp(old - top)
            p = jnp.exp(st - top)
            m_ref[0, i : i + 1, :] = top
            l_ref[0, i : i + 1, :] = l_in[0, i : i + 1, :] * factor + jnp.sum(
                p, axis=0, keepdims=True
            )
            acc_ref[i] = acc_in[i] * factor + dot(vt_scr[g], p.astype(bf16))


def middle_kernel(xt_ref, acc_ref, l_ref, wo_ref, gain_ref, att_ref, mid_ref, n2_ref):
    for h in range(QUERY_HEAD_COUNT):
        g, i = divmod(h, GROUP)
        att_ref[HEAD_DIM * h : HEAD_DIM * (h + 1), :] = (
            acc_ref[h] / l_ref[g, i : i + 1, :]
        ).astype(bf16)
    middle = xt_ref[...].astype(f32) + dot(wo_ref[...], att_ref[...], TN)
    mid_ref[...] = middle
    n2_ref[...] = (middle * inverse_norm(middle) * gain_ref[:, 1:2]).astype(bf16)


def place_cotangent(order_ref, own_ref, got_ref, dst, both):
    core = order_ref[0]
    half = own_ref.shape[2]
    pairs = []
    for k in range(2 if both else 1):
        seq = core if k == 0 else 1 - core
        for ref, at in ((own_ref, core), (got_ref, 1 - core)):
            start = pl.multiple_of(2 * half * k + at * half, 128)
            pairs.append((ref.at[seq], dst.at[:, pl.ds(start, half)]))
    return pairs


def ff_kernel(parts, slots, groups, tile, order_ref, gu_ref, *refs):
    d_pieces, refs = refs[:parts], refs[parts:]
    n2m_ref, n2t_ref, own_ref, got_ref, out_ref, gn_ref, send_ref = refs[:7]
    refs = refs[7:]
    outs = refs[:groups]
    w, wd, n2, n2_t, cot, cot_t, out, gn, grads, gd, sems, out_sems = refs[groups:]
    core = order_ref[0]
    width, ff2 = w.shape
    ff = ff2 // 2
    rows = n2m_ref.shape[1]
    base = 1 + core * slots
    pairs = place_cotangent(order_ref, own_ref, got_ref, cot_t, True)
    pairs.append((n2m_ref, n2_t.at[:, pl.ds(0, rows)]))
    pairs.append((n2t_ref, n2_t.at[:, pl.ds(rows, rows)]))
    early = len(pairs)
    pairs += placed(d_pieces, wd, order_ref, base, ff // parts)
    pairs.append((gu_ref, w))
    copies = run_copies(pairs, sems)
    for copy in copies[:early]:
        copy.wait()
    cot[...] = cot_t[...].T
    n2[...] = n2_t[...].T
    out[...] = jnp.zeros_like(out)
    gn[...] = jnp.zeros_like(gn)
    for copy in copies[early:]:
        copy.wait()
    shard = width // slots

    @pl.loop(0, ff // tile)
    def _(step):
        at = pl.multiple_of(step * tile, tile)
        up_at = pl.multiple_of(ff + step * tile, 128)
        wg = w[:, pl.ds(at, tile)]
        wu = w[:, pl.ds(up_at, tile)]
        w_down = wd[pl.ds(at, tile), :]
        gate = dot(n2[...], wg)
        up = dot(n2[...], wu)
        s = jax.nn.sigmoid(gate)
        swish = gate * s
        hidden = (swish * up).astype(bf16)
        grad_hidden = dot(cot[...], w_down, NT)
        grad_gate = (grad_hidden * up * s * (1.0 + gate * (1.0 - s))).astype(bf16)
        grad_up = (grad_hidden * swish).astype(bf16)
        out[...] += dot(hidden, w_down)
        gn[...] += dot(grad_gate, wg, NT) + dot(grad_up, wu, NT)
        gd[pl.ds(at, tile), :] = dot(hidden, cot[...], TN).astype(bf16)
        g_gate = dot(n2_t[...], grad_gate).astype(bf16)
        g_up = dot(n2_t[...], grad_up).astype(bf16)
        for j in range(slots):
            slot = order_ref[1 + (2 + core) * slots + j]
            grads[slot, :, pl.ds(at, tile)] = g_gate[shard * j : shard * (j + 1)]
            grads[slot, :, pl.ds(up_at, tile)] = g_up[shard * j : shard * (j + 1)]

    per = slots // groups
    down_rows = ff // slots
    for j in range(slots):
        slot = order_ref[1 + (2 + core) * slots + j]
        rows_j = gd[down_rows * j : down_rows * (j + 1), :].astype(f32)
        grads[slot, :, ff2:] = pack_down(rows_j, shard).astype(bf16)
    copies = run_copies(
        [(grads.at[pl.ds(per * k, per)], outs[k]) for k in reversed(range(groups))], out_sems
    )
    out_ref[...] = out[:rows, :].T
    gn_ref[...] = gn[:rows, :].T
    send_ref[:width, :] = out[rows:, :].T.astype(bf16)
    send_ref[width:, :] = gn[rows:, :].T.astype(bf16)
    for copy in copies:
        copy.wait()


def spread(slots, order_ref, part, core, piece, keep_ref, send_ref):
    shard, wide = keep_ref.shape[1], piece.shape[1]
    for keep in range(2):
        ref = keep_ref if keep else send_ref

        @pl.when((core == part) == (keep == 1))
        def _():
            if wide < ref.shape[2]:
                ref[:, :, wide:] = jnp.zeros((slots, shard, ref.shape[2] - wide), bf16)
            for j in range(slots):
                slot = order_ref[1 + (2 + part) * slots + j]
                ref[slot, :, :wide] = piece[shard * j : shard * (j + 1)].astype(bf16)


def turn_kernel(
    slots, order_ref, mid_ref, sum_ref, gn_ref, got_ref, gain_ref, own_cot_ref, got_cot_ref, wo_ref,
    att_ref, acc_ref, m_ref, l_ref,
    fin_ref, gm_ref, og_ref, og_send_ref, do_ref, dot_ref, del_ref, lse_ref, gg_ref, og, gains,
):
    core = order_ref[0]
    step, last = pl.program_id(0), pl.num_programs(0) - 1
    middle = mid_ref[...]
    width = middle.shape[0]
    fin_ref[...] = (middle + sum_ref[...] + got_ref[:width, :].astype(f32)).astype(bf16)
    gn = gn_ref[...] + got_ref[width:, :].astype(f32)
    grad_field, gain_term = norm_back(gn, middle, inverse_norm(middle), gain_ref[:, 1:2])
    gm = jnp.where(step == core, own_cot_ref[0], got_cot_ref[0]).astype(f32) + grad_field
    gm_ref[...] = gm
    low = gm.astype(bf16)
    more = dot(att_ref[...], low, NT)
    gain_term = jnp.broadcast_to(gain_term, gains.shape)

    @pl.when(step == 0)
    def _():
        og[...] = more
        gains[...] = gain_term

    @pl.when(step != 0)
    def _():
        og[...] += more
        gains[...] += gain_term

    ga_t = dot(wo_ref[...], low)
    del_ref[...] = jnp.zeros_like(del_ref)
    lse_ref[...] = m_ref[...] + jnp.log(l_ref[...])
    for h in range(QUERY_HEAD_COUNT):
        g, i = divmod(h, GROUP)
        part = ga_t[HEAD_DIM * h : HEAD_DIM * (h + 1)].astype(bf16)
        dot_ref[h] = part
        wide = part.astype(f32)
        do_ref[h] = wide.T.astype(bf16)
        del_ref[g, i : i + 1, :] = jnp.sum(
            wide * (acc_ref[h] / l_ref[g, i : i + 1, :]), axis=0, keepdims=True
        )

    @pl.when(step == last)
    def _():
        gg_ref[...] = gains[...]
        split = og_ref.shape[2]
        spread(slots, order_ref, 0, core, og[:, :split], og_ref, og_send_ref)
        spread(slots, order_ref, 1, core, og[:, split:], og_ref, og_send_ref)


def backward_kernel(diagonal, first, *refs):
    if first:
        ok_ref, qt_ref, q_ref, dot_ref, do_ref, lse_ref, del_ref, kv_ref, dq_ref, dkv_ref, *scr = refs
        dq_in = None
    else:
        (
            ok_ref, qt_ref, q_ref, dot_ref, do_ref, lse_ref, del_ref, kv_ref, dq_in, dq_ref, dkv_ref, *scr,
        ) = refs
    k_scr, v_scr, kt_scr, dk_scr, dv_scr = scr
    keys = kv_ref.shape[0]
    g = pl.program_id(0)

    @pl.when(ok_ref[0] == 0)
    def _():
        dq_ref[...] = jnp.zeros_like(dq_ref) if first else dq_in[...]
        dkv_ref[...] = jnp.zeros_like(dkv_ref)

    @pl.when(ok_ref[0] != 0)
    def _():
        @pl.when(g == 0)
        def _():
            for j in range(KEY_HEAD_COUNT):
                k = kv_ref[:, HEAD_DIM * j : HEAD_DIM * (j + 1)]
                k_scr[j] = k
                kt_scr[j] = k.astype(f32).T.astype(bf16)
                start = HEAD_DIM * (KEY_HEAD_COUNT + j)
                v_scr[j] = kv_ref[:, start : start + HEAD_DIM]

        parts = 2 if diagonal else 1
        rows = q_ref.shape[1]
        for part in range(parts):
            cols = slice(part * rows // parts, (part + 1) * rows // parts)
            used = (part + 1) * rows // parts if diagonal else keys
            dk = dv = None
            for i in range(GROUP):
                st = dot(k_scr[g, :used, :], qt_ref[i, :, cols])
                p = jnp.exp(st - lse_ref[0, i : i + 1, cols])
                if diagonal:
                    key_at = lax.broadcasted_iota(jnp.int32, st.shape, 0)
                    row_at = lax.broadcasted_iota(jnp.int32, st.shape, 1) + cols.start
                    p = jnp.where(key_at <= row_at, p, 0.0)
                dpt = dot(v_scr[g, :used, :], dot_ref[i, :, cols])
                ds = (p * (dpt - del_ref[0, i : i + 1, cols])).astype(bf16)
                more_v = dot(p.astype(bf16), do_ref[i, cols, :])
                more_k = dot(ds, q_ref[i, cols, :])
                dv = more_v if dv is None else dv + more_v
                dk = more_k if dk is None else dk + more_k
                more_q = dot(kt_scr[g, :, :used], ds)
                if first:
                    dq_ref[i, :, cols] = more_q
                else:
                    dq_ref[i, :, cols] = dq_in[i, :, cols] + more_q
            if part == 0:
                dk_scr[g, :used, :] = dk
                dv_scr[g, :used, :] = dv
            else:
                before = part * rows // parts
                dk_scr[g, :before, :] += dk[:before]
                dv_scr[g, :before, :] += dv[:before]
                dk_scr[g, before:used, :] = dk[before:]
                dv_scr[g, before:used, :] = dv[before:]

        @pl.when(g == KEY_HEAD_COUNT - 1)
        def _():
            dkv_ref[...] = jnp.concatenate(
                [dk_scr[j].astype(bf16) for j in range(KEY_HEAD_COUNT)]
                + [dv_scr[j].astype(bf16) for j in range(KEY_HEAD_COUNT)],
                axis=1,
            )


def last_kernel(
    parts, slots, order_ref, dq_ref, dkv_ref, got_ref, n1t_ref, wq_ref, w_ref, cos_ref, sin_ref,
    xt_ref, gain_ref, gm_ref, gg_two_ref,
    ig_ref, keep_ref, send_ref, dqt_scr, rhs_scr, gn_scr, one, two, gains_scr,
):
    core = order_ref[0]
    step, last = pl.program_id(0), pl.num_programs(0) - 1
    cos, sin = cos_ref[...], sin_ref[...]
    width = dqt_scr.shape[0]
    kv_width = KEY_HEAD_COUNT * HEAD_DIM
    cut = keep_ref.shape[2]
    for h in range(QUERY_HEAD_COUNT):
        at = HEAD_DIM * h
        turned = unrotate_rows(dq_ref[h] * 0.125, cos, sin).astype(bf16)
        dqt_scr[at : at + HEAD_DIM, :] = turned
        if at >= cut:
            rhs_scr[2 * kv_width + at - cut : 2 * kv_width + at - cut + HEAD_DIM, :] = turned
    dkv = (dkv_ref[...].astype(f32) + got_ref[...].astype(f32)).T
    for h in range(KEY_HEAD_COUNT):
        at = HEAD_DIM * h
        rhs_scr[at : at + HEAD_DIM, :] = unrotate_rows(dkv[at : at + HEAD_DIM], cos, sin).astype(
            bf16
        )
    rhs_scr[kv_width : 2 * kv_width, :] = dkv[kv_width:].astype(bf16)
    gn_scr[...] = dot(wq_ref[...], dqt_scr[...])
    rows = width // parts
    for j in range(parts):
        gn_scr[rows * j : rows * (j + 1), :] += dot(
            w_ref[0, j, :kv_width, :], rhs_scr[:kv_width, :], TN
        ) + dot(w_ref[1, j, :kv_width, :], rhs_scr[kv_width : 2 * kv_width, :], TN)
    x = xt_ref[...].astype(f32)
    grad_field, gg_one = norm_back(gn_scr[...], x, inverse_norm(x), gain_ref[:, 0:1])
    ig_ref[...] = (gm_ref[...] + grad_field).astype(bf16)
    more_one = dot(n1t_ref[...], dqt_scr[:cut, :], NT)
    more_two = dot(n1t_ref[...], rhs_scr[...], NT)
    gg_one = jnp.broadcast_to(gg_one, gains_scr.shape)

    @pl.when(step == 0)
    def _():
        one[...] = more_one
        two[...] = more_two
        gains_scr[...] = gg_one

    @pl.when(step != 0)
    def _():
        one[...] += more_one
        two[...] += more_two
        gains_scr[...] += gg_one

    @pl.when(step == last)
    def _():
        free = cut - two.shape[1]
        lane_at = lax.broadcasted_iota(jnp.int32, (width, free), 1)
        gains = jnp.where(
            lane_at == 0, gains_scr[:, 0:1], jnp.where(lane_at == 1, gg_two_ref[:, 0:1], 0.0)
        )
        spread(slots, order_ref, 0, core, one[...], keep_ref, send_ref)
        spread(
            slots, order_ref, 1, core, jnp.concatenate([two[...], gains], axis=1), keep_ref, send_ref
        )


def add_kernel(a_ref, b_ref, *outs):
    for k, out in enumerate(outs):
        if len(outs) == 1:
            out[...] = (a_ref[...].astype(f32) + b_ref[...].astype(f32)).astype(bf16)
        elif out.shape == a_ref.shape[1:]:
            out[...] = (a_ref[k].astype(f32) + b_ref[k].astype(f32)).astype(bf16)
        else:
            at = slice(k * out.shape[0], (k + 1) * out.shape[0])
            out[...] = (a_ref[at].astype(f32) + b_ref[at].astype(f32)).astype(bf16)


def join_kernel(*refs):
    out, refs = refs[-1], refs[:-1]
    block = out.shape[1]
    rows = refs[0].shape[0]
    at = 0
    for a_ref, b_ref in zip(refs[0::2], refs[1::2]):
        cols = a_ref.shape[1]
        total = a_ref[...].astype(f32) + b_ref[...].astype(f32)
        for k in range(out.shape[0]):
            used = max(0, min(block, rows - block * k))
            if used > 0:
                out[k, :used, at : at + cols] = total[block * k : block * k + used].astype(bf16)
            if used < block:
                out[k, used:, at : at + cols] = jnp.zeros((block - used, cols), bf16)
        at += cols


def add_pieces_kernel(chips, order_ref, a_ref, b_ref, *refs):
    outs, scr = refs[:chips], refs[chips]
    step = outs[0].shape[0]
    rows = a_ref.shape[0]
    scr[:rows, :] = a_ref[...].astype(f32) + b_ref[...].astype(f32)
    if rows < scr.shape[0]:
        scr[rows:, :] = jnp.zeros((scr.shape[0] - rows, scr.shape[1]), f32)
    for k in range(chips):
        at = pl.multiple_of(lax.rem(order_ref[1] + k, chips) * step, 16)
        outs[k][...] = scr[pl.ds(at, step), :].astype(bf16)


def sum_kernel(*refs):
    total = refs[0][...].astype(f32)
    for ref in refs[1:-1]:
        total = total + ref[...].astype(f32)
    refs[-1][...] = total.astype(bf16)


def finish_ff_kernel(slots, got_ref, gate_ref, up_ref, down_ref, o_ref, scr):
    shard, ff = gate_ref.shape
    step = ff // slots
    half = step // 2
    width = o_ref.shape[1]
    chips, block = got_ref.shape[0] // 2, got_ref.shape[1]
    packed = ff + ff // 2
    split = got_ref.shape[2] - packed
    for c in range(2):
        for k in range(chips):
            used = max(0, min(block, shard - block * k))
            if used == 0:
                continue
            rows = slice(block * k, block * k + used)
            part = got_ref[2 * k + c].astype(f32)[:used]
            for j in range(slots):
                dst = slice(step * j + half * c, step * j + half * (c + 1))
                gate_ref[rows, dst] = part[:, half * j : half * (j + 1)]
                up_ref[rows, dst] = part[:, ff // 2 + half * j : ff // 2 + half * (j + 1)]
            if c == 0:
                o_ref[rows, :split] = part[:, packed:]
            else:
                o_ref[rows, split:] = part[:, packed : packed + width - split]
            scr[rows, :] = part[:, ff:packed]
        down = unpack_down(scr[:shard, :], width)
        down_ref[:, half * c : half * (c + 1)] = down.T


def finish_kernel(chips, order_ref, *refs):
    mine, theirs = refs[:chips], refs[chips : 2 * chips]
    qg_ref, kg_ref, vg_ref, gg_ref, parts_scr = refs[2 * chips :]
    core = order_ref[0]
    place = order_ref[1]
    step = mine[0].shape[0]
    for k in range(chips):
        at = pl.multiple_of(lax.rem(place + chips - k, chips) * step, 16)
        parts_scr[core, pl.ds(at, step), :] = mine[k][...]
        parts_scr[1 - core, pl.ds(at, step), :] = theirs[k][...]
    shard, width = qg_ref.shape
    kv_width = kg_ref.shape[0]
    cut = parts_scr.shape[2]
    rest = 2 * kv_width + width - cut
    qg_ref[:, :cut] = parts_scr[0, :shard, :].astype(f32)
    qg_ref[:, cut:] = parts_scr[1, :shard, 2 * kv_width : rest].astype(f32)
    kv = parts_scr[1, :, : 2 * kv_width].astype(f32).T
    kg_ref[...] = kv[:kv_width, :shard]
    vg_ref[...] = kv[kv_width:, :shard]
    gg_ref[...] = parts_scr[1, :, rest:].astype(f32).T[:8, :shard]


def moves(fsdp, ctx, target):
    pairs = []
    for f in range(fsdp):
        for c in range(ctx):
            to_f, to_c = target(f, c)
            if 0 <= to_c < ctx:
                pairs.append((f * ctx + c, to_f * ctx + to_c))
    return pairs


def plus(a, b):
    return (a.astype(f32) + b.astype(f32)).astype(bf16)


def program(
    fsdp, ctx,
    block_input, query_weight, key_matrix, value_matrix, out_weight, gate_weight, up_weight,
    down_weight, attention_gain, feedforward_gain, cotangent,
):
    chips = ctx // 2
    paired = fsdp == 4
    sibling = moves(fsdp, ctx, lambda f, c: (f, c ^ 1))
    up_z = moves(fsdp, ctx, lambda f, c: (f, c + 2))
    down_z = moves(fsdp, ctx, lambda f, c: (f, c - 2))
    near = moves(fsdp, ctx, lambda f, c: (f ^ (1 + c % 2), c))
    far = moves(fsdp, ctx, lambda f, c: (f ^ (2 - c % 2), c))
    rotations = [
        moves(fsdp, ctx, lambda f, c, k=k: (f, (c + 2 * k) % ctx)) for k in range(chips)
    ]
    columns = [[c + 2 * z for z in range(chips)] for c in range(2)]
    rank = lax.axis_index("ctx")
    core, place = rank % 2, rank // 2
    spot = lax.axis_index("fsdp")
    _, half, width = block_input.shape
    rows = 2 * half
    kv_width = KEY_HEAD_COUNT * HEAD_DIM
    shard = width // fsdp
    ff = gate_weight.shape[1]
    parts = fsdp if paired else 1

    def send(value, pairs):
        return lax.ppermute(value, AXES, pairs)

    ids = jnp.arange(fsdp, dtype=jnp.int32)
    if paired:
        first_order = jnp.bitwise_xor(spot, ids)
        second_order = jnp.bitwise_xor(spot, jnp.array([0, 2, 1, 3], jnp.int32))
        second_slot = jnp.where(first_order == 1, 2, jnp.where(first_order == 2, 1, first_order))
        order = [core[None], first_order, second_order, first_order, second_slot]
    else:
        order = [core[None], ids, ids, ids, ids]
    order = jnp.concatenate([o.astype(jnp.int32) for o in order])
    where = jnp.stack([core, place]).astype(jnp.int32)

    def gather(item, axis=0):
        if not paired:
            return [lax.all_gather(item, "fsdp", axis=axis, tiled=True)]
        a = send(item, near)
        b = send(item, far)
        return [item, a, b, send(a, far)]

    x_t = jnp.transpose(block_input, (0, 2, 1))
    cot_t = jnp.transpose(cotangent, (0, 2, 1))

    gains = jnp.pad(jnp.stack([attention_gain, feedforward_gain]), ((0, 14), (0, 0)))
    item, x_send = call(
        first_kernel,
        [((kv_width + 16, shard), bf16), ((width, half), bf16)],
        (where, x_t, key_matrix.T, value_matrix.T, gains),
        0,
        scratch=[pltpu.SemaphoreType.DMA],
        smem=1,
        hbm=(1,),
    )
    x_got = send(x_send, sibling)
    if paired:
        near_got = send(item, near)
        far_got = send(item, far)
        mine = [item, near_got, far_got, send(near_got, far)]
    else:
        mine = gather(item, axis=1)
    theirs = [send(piece, sibling) for piece in mine]
    positions = (place * rows + jnp.arange(rows, dtype=jnp.int32)).astype(f32)
    steps = jnp.arange(HEAD_DIM // 2, dtype=f32)
    angles = (rope_base ** (-2.0 * steps / HEAD_DIM))[:, None] * positions[None, :]
    cos, sin = jnp.cos(angles), jnp.sin(angles)

    xt, n1t, kv, w_kv, gain = call(
        functools.partial(key_kernel, parts, fsdp),
        [
            ((width, rows), bf16),
            ((width, rows), bf16),
            ((rows, 2 * kv_width), bf16),
            ((2, parts, kv_width + 16, width // parts), bf16),
            ((width, 8), f32),
        ],
        (order, x_t, x_got, cos, sin, *mine, *theirs),
        5,
        scratch=[pltpu.SemaphoreType.DMA((2 + 2 * parts,))],
        smem=1,
        hbm=(1, 2, *range(5, 5 + 2 * parts)),
    )
    qo_item, gu_item, down_item = call(
        functools.partial(halves_kernel, fsdp),
        [
            ((shard, width), bf16),
            ((shard, ff), bf16),
            ((down_weight.shape[0] // 2, width), bf16),
        ],
        (where, query_weight, out_weight, gate_weight, up_weight, down_weight.T),
        3,
        smem=1,
        after=(kv,),
    )
    gate_up = lax.all_gather(gu_item, "fsdp", axis=0, tiled=True)

    stat = ((KEY_HEAD_COUNT, 8, rows), f32)
    acc_shape = ((QUERY_HEAD_COUNT, HEAD_DIM, rows), f32)
    key_scratch = pltpu.VMEM((KEY_HEAD_COUNT, rows, HEAD_DIM), bf16)
    turned_scratch = pltpu.VMEM((KEY_HEAD_COUNT, HEAD_DIM, rows), bf16)
    wide_scratch = pltpu.VMEM((KEY_HEAD_COUNT, rows, HEAD_DIM), f32)

    def ok(distance):
        return (place >= distance).astype(jnp.int32)[None]

    def heads(array):
        return leading(array, array.shape[0] // KEY_HEAD_COUNT)

    cot_got = send(cot_t, sibling)
    blocks = [kv]
    blocks.append(send(kv, up_z))
    mine = gather(qo_item)
    theirs = [send(piece, sibling) for piece in mine]
    qt, q, wq, wo = call(
        functools.partial(query_kernel, parts, fsdp),
        [
            ((QUERY_HEAD_COUNT, HEAD_DIM, rows), bf16),
            ((QUERY_HEAD_COUNT, rows, HEAD_DIM), bf16),
            ((width, width), bf16),
            ((width, width), bf16),
        ],
        (order, n1t, cos, sin, *mine, *theirs),
        5,
        scratch=[pltpu.SemaphoreType.DMA((2 * parts,))],
        smem=1,
        hbm=range(4, 4 + 2 * parts),
    )
    down_pieces = gather(down_item)
    states = [heads(Out(*stat)), heads(Out(*stat)), heads(Out(*acc_shape))]
    m, l, acc = call_grid(
        forward_diagonal,
        KEY_HEAD_COUNT,
        states,
        (ok(0), heads(qt), whole(kv)),
        8,
        scratch=[key_scratch, turned_scratch],
    )
    for distance in range(1, chips):
        if distance + 1 < chips:
            blocks.append(send(blocks[distance], up_z))
        m, l, acc = call_grid(
            forward_full,
            KEY_HEAD_COUNT,
            states,
            (ok(distance), heads(qt), whole(blocks[distance]), heads(m), heads(l), heads(acc)),
            10,
            scratch=[key_scratch, turned_scratch],
            after=(cot_got, *down_pieces[1:3]) if distance == chips - 1 else (),
        )

    att, middle, n2 = call(
        middle_kernel,
        [((width, rows), bf16), ((width, rows), f32), ((width, rows), bf16)],
        (xt, acc, l, wo, gain),
        4,
        after=down_pieces[3:],
    )

    n2_got = send(n2, sibling)
    groups = 2 if paired else 1
    per = fsdp // groups
    half_ff = ff // 2
    tile = 256
    ff_out = call(
        functools.partial(ff_kernel, parts, fsdp, groups, tile),
        [((width, rows), f32), ((width, rows), f32), ((2 * width, rows), bf16)]
        + [((per, shard, ff + half_ff), bf16)] * groups,
        (order, gate_up, *down_pieces, n2, n2_got, cot_t, cot_got),
        37,
        scratch=[
            pltpu.VMEM((width, ff), bf16),
            pltpu.VMEM((half_ff, width), bf16),
            pltpu.VMEM((2 * rows, width), bf16),
            pltpu.VMEM((width, 2 * rows), bf16),
            pltpu.VMEM((2 * rows, width), bf16),
            pltpu.VMEM((width, 2 * rows), bf16),
            pltpu.VMEM((2 * rows, width), f32),
            pltpu.VMEM((2 * rows, width), f32),
            pltpu.VMEM((fsdp, shard, ff + half_ff), bf16),
            pltpu.VMEM((half_ff, width), bf16),
            pltpu.SemaphoreType.DMA((7 + parts,)),
            pltpu.SemaphoreType.DMA((groups,)),
        ],
        smem=1,
        hbm=range(1, 6 + parts),
        outs_hbm=range(3, 3 + groups),
        vmem=LARGE,
    )
    ff_sum, gn, ff_send = ff_out[:3]
    ff_terms = ff_out[3:]
    ff_got = send(ff_send, sibling)

    split = 512
    if paired:
        ff_far = send(ff_terms[1], far)

    def one_half(array):
        return trailing(array, half)

    def cot_of(array, mine):
        return (array, (1, width, half), lambda i, s: (s[0], 0, 0))

    fin, grad_middle, o_keep, o_send, do, dot_t, delta, lse, gain_two_term = call_grid(
        functools.partial(turn_kernel, fsdp),
        2,
        [
            one_half(Out((width, rows), bf16)),
            one_half(Out((width, rows), f32)),
            whole(Out((fsdp, shard, split), bf16)),
            whole(Out((fsdp, shard, split), bf16)),
            (
                Out((QUERY_HEAD_COUNT, rows, HEAD_DIM), bf16),
                (QUERY_HEAD_COUNT, half, HEAD_DIM),
                lambda i, s: (0, i, 0),
            ),
            one_half(Out((QUERY_HEAD_COUNT, HEAD_DIM, rows), bf16)),
            one_half(Out(*stat)),
            one_half(Out(*stat)),
            whole(Out((width, 8), f32)),
        ],
        (
            order, one_half(middle), one_half(ff_sum), one_half(gn), one_half(ff_got), whole(gain),
            cot_of(cot_t, True), cot_of(cot_got, False), whole(wo), one_half(att), one_half(acc),
            one_half(m), one_half(l),
        ),
        11,
        scratch=[pltpu.VMEM((width, width), f32), pltpu.VMEM((width, 8), f32)],
    )

    def added(a, b, count, after=()):
        lead = a.shape[0] // count
        shape = a.shape if count == 1 else (a.shape[1:] if lead == 1 else (lead, *a.shape[1:]))
        return call(add_kernel, [(shape, bf16)] * count, (a, b), 2, after=after)

    def scatter_row(terms):
        return lax.psum_scatter(terms[0], "fsdp", scatter_dimension=0, tiled=False)

    block = -(-shard // (16 * chips)) * 16

    def scatter_column(pairs, after=()):
        shape = (chips, block, sum(a.shape[1] for a in pairs[::2]))
        (cut_up,) = call(join_kernel, [(shape, bf16)], pairs, 3, after=after)
        part = lax.psum_scatter(
            cut_up, "ctx", scatter_dimension=0, tiled=False, axis_index_groups=columns
        )
        return cut_up, part

    def pull(distance, dq, after):
        first = dq is None
        args = [
            ok(distance), heads(qt), heads(q), heads(dot_t), heads(do), heads(lse), heads(delta),
            whole(blocks[distance]),
        ]
        return call_grid(
            functools.partial(backward_kernel, distance == 0, first),
            KEY_HEAD_COUNT,
            [heads(Out(*acc_shape)), whole(Out((rows, 2 * kv_width), bf16))],
            args if first else args + [heads(dq)],
            14,
            scratch=[key_scratch, key_scratch, turned_scratch, wide_scratch, wide_scratch],
            after=after,
        )

    o_got = send(o_send, sibling)
    dq, dkv = pull(chips - 1, None, ())
    if not paired:
        halves = [scatter_row(ff_terms), scatter_row(added(o_keep, o_got, 1))]
        pairs = [a for term in halves for a in (term, jnp.zeros_like(term))]
        joined, part = scatter_column(pairs)
    waits = ()
    for distance in reversed(range(1, chips)):
        coming = send(dkv, down_z)
        done = chips - 1 - distance
        if paired and done == 0:
            o_terms = added(o_keep, o_got, 2, (dq,))
            o_far = send(o_terms[1], far)
            waits += (o_terms[1],)
        if paired and done == 1:
            ff_half = added(ff_terms[0], ff_far, 2, (dq,))
            ff_back = send(ff_half[1], near)
            o_half = added(o_terms[0], o_far, 2, (dq,))
            o_back = send(o_half[1], near)
            waits += (ff_half[1], o_half[1])
        if paired and distance == 1:
            joined, part = scatter_column((ff_half[0], ff_back, o_half[0], o_back), (dq, dkv))
            waits += (joined,)
        dq, dkv = pull(distance - 1, dq, waits)
        waits = ()
        if distance > 1:
            (dkv,) = added(dkv, coming, 1)
            waits = (dkv,)

    cut = 896
    rest = 2 * kv_width + width - cut
    input_grad, keep, other = call_grid(
        functools.partial(last_kernel, parts, fsdp),
        2,
        [
            one_half(Out((width, rows), bf16)),
            whole(Out((fsdp, shard, cut), bf16)),
            whole(Out((fsdp, shard, cut), bf16)),
        ],
        (
            order, one_half(dq), leading(dkv, half), leading(coming, half), one_half(n1t), whole(wq),
            whole(w_kv), one_half(cos), one_half(sin), one_half(xt), whole(gain),
            one_half(grad_middle), whole(gain_two_term),
        ),
        9,
        scratch=[
            pltpu.VMEM((width, half), bf16),
            pltpu.VMEM((rest, half), bf16),
            pltpu.VMEM((width, half), f32),
            pltpu.VMEM((width, cut), f32),
            pltpu.VMEM((width, rest), f32),
            pltpu.VMEM((width, 8), f32),
        ],
    )
    (part,) = call(sum_kernel, [(part.shape, bf16)], (part,), 1, after=(keep,))
    ff_total = lax.all_gather(part, "ctx", axis=0, tiled=False)
    other = send(other, sibling)
    if paired:
        terms = added(keep, other, 2)
        a, b = added(terms[0], send(terms[1], far), 2)
        b = send(b, near)
    else:
        a = scatter_row(added(keep, other, 1))
        b = jnp.zeros_like(a)

    pieces = call(
        functools.partial(add_pieces_kernel, chips),
        [((block, cut), bf16)] * chips,
        (where, a, b),
        1,
        scratch=[pltpu.VMEM((block * chips, cut), f32)],
        smem=1,
    )
    got = [send(pieces[k], rotations[k]) for k in range(1, chips)]
    (total,) = call(sum_kernel, [((block, cut), bf16)], (pieces[0], *got), 1)
    pieces = [total] + [send(total, rotations[k]) for k in range(1, chips)]
    other_pieces = [send(piece, sibling) for piece in pieces]
    query_grad, key_grad, value_grad, gain_grads = call(
        functools.partial(finish_kernel, chips),
        [
            ((shard, width), f32),
            ((kv_width, shard), f32),
            ((kv_width, shard), f32),
            ((8, shard), f32),
        ],
        (where, *pieces, *other_pieces),
        1,
        scratch=[pltpu.VMEM((2, block * chips, cut), bf16)],
        smem=1,
    )
    gate_grad, up_grad, down_grad, out_grad = call(
        functools.partial(finish_ff_kernel, fsdp),
        [
            ((shard, ff), f32),
            ((shard, ff), f32),
            ((width, ff // fsdp), f32),
            ((shard, width), f32),
        ],
        (ff_total,),
        1,
        scratch=[pltpu.VMEM((block * chips, half_ff), f32)],
    )

    def scatter_sequence(block):
        keep = lax.dynamic_slice_in_dim(block, core * half, half, 1)
        got = send(lax.dynamic_slice_in_dim(block, (1 - core) * half, half, 1), sibling)
        both = jnp.stack([jnp.where(core == 0, keep, got), jnp.where(core == 0, got, keep)])
        return jnp.transpose(both, (0, 2, 1))

    return (
        scatter_sequence(fin),
        scatter_sequence(input_grad),
        query_grad,
        key_grad.T,
        value_grad.T,
        out_grad,
        gate_grad,
        up_grad,
        down_grad.T,
        gain_grads[0],
        gain_grads[1],
    )


def solution(mesh):
    in_specs = (
        P("fsdp", "ctx", None),
        P("fsdp", None),
        P("fsdp", None),
        P("fsdp", None),
        P("fsdp", None),
        P("fsdp", None),
        P("fsdp", None),
        P("fsdp", None),
        P("fsdp"),
        P("fsdp"),
        P("fsdp", "ctx", None),
    )
    out_specs = (
        P("fsdp", "ctx", None),
        P("fsdp", "ctx", None),
        P("fsdp", None),
        P("fsdp", None),
        P("fsdp", None),
        P("fsdp", None),
        P("fsdp", None),
        P("fsdp", None),
        P("fsdp", None),
        P("fsdp"),
        P("fsdp"),
    )
    body = functools.partial(program, mesh.shape["fsdp"], mesh.shape["ctx"])
    return jax.shard_map(body, mesh=mesh, in_specs=in_specs, out_specs=out_specs, check_vma=False)
```
